512 devices in a mesh: dp: 16 (over y_lo, z), seq: 32 (over y_hi, x, core).
Axes of the slice: x: 4, y: 8 (y_hi: 4, y_lo: 2; y = y_hi * 2 + y_lo), z: 8, core: 2. Of those that a mesh axis runs over, the one named last changes fastest.
Arguments:
- queries: bfloat16 [16, 4096, 512], P('dp', 'seq'), may hold values from -6 to 6
- keys: bfloat16 [16, 4096, 512], P('dp', 'seq'), may hold values from -6 to 6
- values: bfloat16 [16, 4096, 512], P('dp', 'seq'), may hold values from -6 to 6
- gates: bfloat16 [16, 4096, 512], P('dp', 'seq'), may hold values from -6 to 6
- out_proj: bfloat16 [512, 1024], replicated, may hold values from -0.25 to 0.25
- out_grad: bfloat16 [16, 4096, 1024], P('dp', 'seq'), may hold values from -6 to 6
- lengths: int32 [16, 4], P('dp'), may hold values from 1 to 2048, 4096 in all within a row
- rel_bias: float32 [4, 16], replicated, may hold values from -2 to 2
Outputs:
- projected: bfloat16 [16, 4096, 1024], P('dp', 'seq')
- query_grad: bfloat16 [16, 4096, 512], P('dp', 'seq')
- key_grad: bfloat16 [16, 4096, 512], P('dp', 'seq')
- value_grad: bfloat16 [16, 4096, 512], P('dp', 'seq')
- bias_grad: float32 [4, 16], replicated
The draws below stay inside these ranges and needn't reach their ends.
Inputs may be any that keep to these rules, and one draw needn't show every extreme that they name: In every data row the 4 lengths sum to 4096 and the longest is exactly half of 4096.
All inputs are finite; a program needn't handle non-finite values.
Results may differ from the reference program's by a relative error of at most 0.0059.
Values may be sent and summed in bfloat16 or wider, within the bound.
A program may use at most 64 MiB of HBM per device.

```python
import math
import jax
import jax.numpy as jnp
import numpy as np
from jax import lax

H = 4
D = 1024
BUCKETS = 16
USERS = 4
L = 4096
HD = 512
ROWS = 16


def level_of(own_key, shape, cuts, low, largest):
    gain, own = 1.0, jax.random.fold_in(own_key, 6)
    for axis_at, blocks in cuts:
        steps = jnp.exp(jax.random.uniform(jax.random.fold_in(own, axis_at), (blocks,), jnp.float32, low / len(cuts), largest / len(cuts)))
        gain = gain * jnp.repeat(steps, shape[axis_at] // blocks).reshape([-1 if axis == axis_at else 1 for axis in range(len(shape))])
    return gain


def profile(amount, total, reach, lean):
    weights = [(1 << 20) // math.isqrt(grade ** lean) + 1 for grade in range(2, amount + 1)]
    spare, holding = total - reach - (amount - 1), [1] * (amount - 1)
    while spare > 0:
        movable = [i for i in range(amount - 1) if holding[i] < reach]
        mass, budget = sum([weights[i] for i in movable]), spare
        for i in movable:
            extra = min(reach - holding[i], max(1, budget * weights[i] // mass), spare)
            holding[i] = holding[i] + extra
            spare = spare - extra
    return np.array([reach] + holding)


def ragged_sizes(rng, number_of, total, most, lean):
    if number_of == 2:
        one = jax.random.randint(rng, (), max(1, total - most), min(most, total - 1) + 1)
        return jnp.stack([one, total - one])
    sizes = jnp.asarray(profile(number_of, total, most, lean), jnp.int32)
    pairs = (number_of - 1) // 2
    giver, taker = sizes[1:1 + 2 * pairs:2], sizes[2:2 + 2 * pairs:2]
    room = jnp.minimum(giver - 1, most - taker)
    moved = jax.random.randint(jax.random.fold_in(rng, 1), (pairs,), 0, 1 << 20) % (room + 1)
    sizes = sizes.at[1:1 + 2 * pairs:2].set(giver - moved).at[2:2 + 2 * pairs:2].set(taker + moved)
    return sizes[jax.random.permutation(jax.random.fold_in(rng, 2), number_of)]


def normal_values(key, extent, scale, bound, shards=(), kind=jnp.bfloat16):
    factor_of = level_of(key, extent, shards, -0.22, 0.18) if shards else 1.0
    drawn = jax.random.normal(key, extent, jnp.float32) * scale * factor_of
    return jnp.minimum(jnp.maximum(drawn, -bound), bound).astype(kind)


def setup_inputs(seed: int = 0) -> dict:
    streams_of = jax.random.split(jax.random.key(seed), 9)
    queries = normal_values(streams_of[0], (ROWS, L, HD), 1.0, 6.0, ((0, 16), (1, 32)))
    keys = normal_values(streams_of[1], (ROWS, L, HD), 1.0, 6.0, ((0, 16), (1, 32)))
    values = normal_values(streams_of[2], (ROWS, L, HD), 1.0, 6.0, ((0, 16), (1, 32)))
    gates = normal_values(streams_of[3], (ROWS, L, HD), 1.0, 6.0, ((0, 16), (1, 32)))
    out_proj = normal_values(streams_of[4], (HD, D), HD ** -0.5, 0.25)
    out_grad = normal_values(streams_of[5], (ROWS, L, D), 1.0, 6.0, ((0, 16), (1, 32)))
    lengths = jax.vmap(lambda own: ragged_sizes(own, USERS, L, L // 2, 2))(jax.random.split(streams_of[6], ROWS)).reshape((ROWS, USERS)).astype(jnp.int32)
    rel_bias = jnp.clip(jax.random.uniform(streams_of[7], (H, BUCKETS), jnp.float32, -2.0, 2.0), -2.0, 2.0)
    return dict(queries=queries, keys=keys, values=values, gates=gates, out_proj=out_proj, out_grad=out_grad, lengths=lengths, rel_bias=rel_bias)


epsilon = 1e-05

def rounded(array):
    return lax.optimization_barrier(array.astype(jnp.bfloat16)).astype(jnp.float32)

def bucket_of(distance):
    bucket = jnp.zeros(distance.shape, jnp.int32)
    for octave in range(15):
        bucket = bucket + (distance >= 2 ** octave).astype(jnp.int32)
    return bucket

def one_row(queries, keys, values, gates, out_grad, lengths_row, rel_bias, out_proj):
    row_total = queries.shape[0]
    heads = rel_bias.shape[0]
    head_width = queries.shape[1] // heads
    scale = head_width ** (-0.5)
    query_heads = queries.reshape(row_total, heads, head_width).astype(jnp.float32)
    key_heads = keys.reshape(row_total, heads, head_width).astype(jnp.float32)
    value_heads = values.reshape(row_total, heads, head_width).astype(jnp.float32)
    gate_heads = gates.reshape(row_total, heads, head_width).astype(jnp.float32)
    ends = jnp.cumsum(lengths_row).astype(jnp.int32)
    position = jnp.arange(row_total, dtype=jnp.int32)
    segment = lax.optimization_barrier(jnp.sum((position[:, None] >= ends[None, :]).astype(jnp.int32), axis=1))
    block_rows = min(512, row_total)
    block_count = row_total // block_rows

    def scores_of(block_index):
        first = block_index * block_rows
        query_block = lax.dynamic_slice_in_dim(query_heads, first, block_rows, 0)
        query_pos = lax.dynamic_slice_in_dim(position, first, block_rows, 0)
        query_seg = lax.dynamic_slice_in_dim(segment, first, block_rows, 0)
        distance = query_pos[:, None] - position[None, :]
        bucket = bucket_of(distance)
        scores = jnp.einsum('qhd,khd->hqk', query_block, key_heads) * scale + rel_bias[:, bucket]
        allowed = (query_seg[:, None] == segment[None, :]) & (distance >= 0)
        return (scores, allowed[None], bucket, query_block)

    def forward_block(block_index):
        scores, allowed, bucket, query_block = scores_of(block_index)
        weights = rounded(jnp.where(allowed, jax.nn.silu(scores), 0.0))
        return jnp.einsum('hqk,khd->qhd', weights, value_heads)
    indices = jnp.arange(block_count, dtype=jnp.int32)
    mixed = lax.map(forward_block, indices).reshape(row_total, heads, head_width)
    average = lax.optimization_barrier(jnp.mean(mixed, axis=2, keepdims=True))
    centred = mixed - average
    variance = lax.optimization_barrier(jnp.mean(centred * centred, axis=2, keepdims=True))
    inverse = lax.rsqrt(variance + epsilon)
    normed = centred * inverse
    gated = (normed * gate_heads).astype(jnp.bfloat16).reshape(row_total, heads * head_width)
    projected = jnp.dot(gated, out_proj, preferred_element_type=jnp.float32).astype(jnp.bfloat16)
    gated_grad = jnp.dot(out_grad, out_proj.T, preferred_element_type=jnp.float32)
    normed_grad = gated_grad.reshape(row_total, heads, head_width) * gate_heads
    mixed_grad = (normed_grad - lax.optimization_barrier(jnp.mean(normed_grad, axis=2, keepdims=True)) - normed * lax.optimization_barrier(jnp.mean(normed_grad * normed, axis=2, keepdims=True))) * inverse
    mixed_grad = rounded(mixed_grad)

    def backward_block(carry, block_index):
        key_grad, value_grad, bias_grad = carry
        scores, allowed, bucket, query_block = scores_of(block_index)
        grad_block = lax.dynamic_slice_in_dim(mixed_grad, block_index * block_rows, block_rows, 0)
        sigmoid_s = jax.nn.sigmoid(scores)
        weights = rounded(jnp.where(allowed, scores * sigmoid_s, 0.0))
        attn_grad = jnp.einsum('qhd,khd->hqk', grad_block, value_heads)
        score_grad = jnp.where(allowed, attn_grad * sigmoid_s * (1.0 + scores * (1.0 - sigmoid_s)), 0.0)
        score_low = rounded(score_grad)
        query_part = jnp.einsum('hqk,khd->qhd', score_low, key_heads)
        key_grad = key_grad + jnp.einsum('hqk,qhd->khd', score_low, query_block)
        value_grad = value_grad + jnp.einsum('hqk,qhd->khd', weights, grad_block)
        bias_terms = [lax.optimization_barrier(jnp.sum(jnp.where(bucket[None] == octave, score_grad, 0.0), axis=(1, 2))) for octave in range(rel_bias.shape[1])]
        bias_grad = bias_grad + jnp.stack(bias_terms, axis=1)
        return ((key_grad, value_grad, bias_grad), query_part)
    start_carry = (jnp.zeros((row_total, heads, head_width), jnp.float32), jnp.zeros((row_total, heads, head_width), jnp.float32), jnp.zeros(rel_bias.shape, jnp.float32))
    (key_grad, value_grad, bias_grad), query_parts = lax.scan(backward_block, start_carry, indices)
    query_grad = query_parts.reshape(row_total, heads * head_width).astype(jnp.bfloat16)
    key_grad = key_grad.reshape(row_total, heads * head_width).astype(jnp.bfloat16)
    value_grad = value_grad.reshape(row_total, heads * head_width).astype(jnp.bfloat16)
    return (projected, query_grad, key_grad, value_grad, bias_grad)

def reference(queries, keys, values, gates, out_proj, out_grad, lengths, rel_bias):

    def per_row(members):
        return one_row(members[0], members[1], members[2], members[3], members[4], members[5], rel_bias, out_proj)
    projected, query_grad, key_grad, value_grad, bias_rows = lax.map(per_row, (queries, keys, values, gates, out_grad, lengths))
    return (projected, query_grad, key_grad, value_grad, lax.optimization_barrier(jnp.sum(bias_rows, axis=0)))
```

```python
import jax
import jax.numpy as jnp
from jax import lax
from jax.experimental import pallas as pl
from jax.experimental.pallas import tpu as pltpu
from jax.sharding import PartitionSpec as P

F32 = jnp.float32
BF16 = jnp.bfloat16
EPS = 1e-05
NEG = -1e5
HALF_SCALE = 0.5 * 128 ** (-0.5)
FAR = 1 << 20
TABLED = (0, 1, 2, 4)
LEFT, DIAG, RIGHT = 1, 2, 3


def dot_nt(a, b):
    return lax.dot_general(a, b, (((1,), (1,)), ((), ())), preferred_element_type=F32)


def dot_nn(a, b):
    return jnp.dot(a, b, preferred_element_type=F32)


def kernel(
    q_in, k_in, v_in, gates_in, proj_in, og_in, len_ref, rb_ref,
    projected_ref, dq_ref, dk_ref, dv_ref, bias_ref,
    kbuf, vbuf, qbuf, gbuf, ngbuf, ngsrc, nrmsrc, nrmbuf, lensrc, lenbuf,
    og_vm, gates_vm, proj_vm, gated_vm, outproj_vm,
    tab_q, tab_k, st_t, en_t, acc_m, acc_q, acc_k, acc_v,
    out_q, out_k, out_v, acc_bias, acc_far, red,
    send_sems, y_sems, x_sems, ret_sems, red_sems, len_sem, local_sems,
):
    dp = lax.axis_index("dp")
    seq = lax.axis_index("seq")
    ylo, z = lax.div(dp, 8), lax.rem(dp, 8)
    yh, xc = lax.div(seq, 8), lax.rem(seq, 8)
    x, c = lax.div(xc, 2), lax.rem(xc, 2)
    odp = lax.rem(dp + 8, 16)
    yi = ylo * 4 + yh

    def place(rel):
        return lax.rem(x + rel, 4)

    left, right, diag = place(3), place(1), place(2)
    dev_left = (dp, yh * 8 + left * 2 + c)
    dev_right = (dp, yh * 8 + right * 2 + c)
    dev_sib = (dp, yh * 8 + x * 2 + 1 - c)

    def z_partner(k):
        other = lax.rem(z + k, 8)
        return (ylo * 8 + other, seq), other

    def xc_partner(k):
        other = lax.rem(xc + k, 8)
        return (dp, yh * 8 + other), other

    def y_partner(k):
        other = lax.rem(yi + k, 8)
        return (lax.div(other, 4) * 8 + z, lax.rem(other, 4) * 8 + xc), other

    partners = (z_partner, xc_partner, y_partner)

    barrier = pltpu.get_barrier_semaphore()
    for partner in (y_partner, xc_partner, z_partner):
        for k in range(1, 8):
            pl.semaphore_signal(
                barrier, inc=1, device_id=partner(k)[0], device_id_type=pl.DeviceIdType.MESH
            )

    local = [
        pltpu.make_async_copy(og_in.at[0], og_vm, local_sems.at[0]),
        pltpu.make_async_copy(proj_in, proj_vm, local_sems.at[1]),
        pltpu.make_async_copy(gates_in.at[0], gates_vm, local_sems.at[2]),
    ]
    ends = []
    total = len_ref[0, 0]
    ends.append(total)
    for u in range(1, 4):
        total = total + len_ref[0, u]
        ends.append(total)
    row_at = lax.broadcasted_iota(jnp.int32, (8, 128), 0)
    end_rows = jnp.zeros((8, 128), F32)
    for u in range(4):
        end_rows = jnp.where(row_at == u, ends[u].astype(F32), end_rows)
    lensrc[...] = end_rows

    pending = []

    def send(src, dst, recv_sem, dev):
        copy = pltpu.make_async_remote_copy(
            src_ref=src, dst_ref=dst, send_sem=send_sems.at[len(pending)], recv_sem=recv_sem,
            device_id=dev, device_id_type=pl.DeviceIdType.MESH,
        )
        copy.start()
        pending.append(copy)

    def arrived(dst, sem):
        pltpu.make_async_copy(dst, dst, sem).wait()

    pl.semaphore_wait(barrier, 21)

    def y_send(a, src_of, dst):
        for h in range(4):
            send(src_of(h), dst, y_sems.at[a, yh], (odp, h * 8 + xc))

    def y_wait(a, dst_of):
        for s in range(4):
            arrived(dst_of(s), y_sems.at[a, s])

    for a, (src, buf) in enumerate(((k_in, kbuf), (v_in, vbuf), (q_in, qbuf))):
        y_send(a, lambda h, src=src: src.at[0, :, h * 128 : (h + 1) * 128], buf.at[yh, xc])
        if a == 0:
            send(lensrc, lenbuf, len_sem.at[0], (odp, seq))
    for copy in local:
        copy.start()

    def piece(buf, half, at):
        return buf.at[pl.ds(2 * half, 2), at]

    def own_of(at):
        return at * 2 + c

    def x_start(a, buf):
        mine = own_of(x)
        send(piece(buf, 0, mine), piece(buf, 0, mine), x_sems.at[a, 0], dev_right)
        send(piece(buf, 1, mine), piece(buf, 1, mine), x_sems.at[a, 3], dev_left)
        send(piece(buf, 1, mine), piece(buf, 1, mine), x_sems.at[a, 1], dev_right)
        send(piece(buf, 0, mine), piece(buf, 0, mine), x_sems.at[a, 4], dev_left)
        send(buf.at[:, mine], buf.at[:, mine], x_sems.at[a, 6], dev_sib)

    def x_pass(a, buf, steps):
        for half, whose, slot, to in steps:
            part = piece(buf, half, own_of(whose))
            arrived(part, x_sems.at[a, slot])
            if to is not None:
                device, next_slot = to
                send(part, part, x_sems.at[a, next_slot], device)
            send(part, part, x_sems.at[a, slot + 7], dev_sib)

    def x_near(a, buf):
        x_pass(a, buf, ((0, left, 0, (dev_right, 2)), (1, right, 3, (dev_left, 5))))

    def x_rest(a, buf):
        x_pass(a, buf, ((1, left, 1, None), (0, right, 4, None)))

    def x_far(a, buf):
        x_pass(a, buf, ((0, diag, 2, None), (1, diag, 5, None)))

    def sib_of(at):
        return at * 2 + 1 - c

    def sib_own(a, buf):
        arrived(buf.at[:, sib_of(x)], x_sems.at[a, 6])

    def sib_near(a, buf):
        arrived(piece(buf, 0, sib_of(left)), x_sems.at[a, 7])
        arrived(piece(buf, 1, sib_of(right)), x_sems.at[a, 10])
        arrived(piece(buf, 1, sib_of(left)), x_sems.at[a, 8])
        arrived(piece(buf, 0, sib_of(right)), x_sems.at[a, 11])

    def sib_far(a, buf):
        arrived(piece(buf, 0, sib_of(diag)), x_sems.at[a, 9])
        arrived(piece(buf, 1, sib_of(diag)), x_sems.at[a, 12])

    wide = (128, 256)
    sub = lax.broadcasted_iota(jnp.int32, wide, 0)
    lane = lax.broadcasted_iota(jnp.int32, wide, 1)
    dist_q = 128 * c + sub - lane
    dist_k = lane - sub - 128 * c
    half_bias = [0.5 * rb_ref[yh, b] for b in range(12)]

    def biases(dist, low, high):
        filled = jnp.full(wide, half_bias[low], F32)
        for b in range(low + 1, high + 1):
            filled = jnp.where(dist >= 2 ** (b - 1), half_bias[b], filled)
        return filled

    spans = {0: (0, 9), 1: (1, 9), 2: (9, 10), 4: (10, 11)}

    def build_tables():
        for tab, dist in ((tab_q, dist_q), (tab_k, dist_k)):
            for at, d in enumerate(TABLED):
                filled = biases(dist + 256 * d, *spans[d])
                if d == 0:
                    filled = jnp.where(dist >= 0, filled, NEG)
                tab[at] = filled

    def bias_at(tab, d):
        if d in TABLED:
            return tab[TABLED.index(d)]
        return half_bias[10 if d == 3 else 11]

    def build_bounds():
        arrived(lenbuf, len_sem.at[0])
        sub_f, lane_f = sub.astype(F32), lane.astype(F32)
        ends_at = [jnp.broadcast_to(lenbuf[u : u + 1, 0:1], wide) for u in range(4)]
        for y in range(4):
            pos = sub_f + ((8 * y + xc) * 128).astype(F32)
            start = jnp.zeros(wide, F32)
            end = ends_at[3]
            for u in (0, 1, 2):
                start = jnp.where(pos >= ends_at[u], ends_at[u], start)
            for u in (2, 1, 0):
                end = jnp.where(pos < ends_at[u], ends_at[u], end)
            st_t[y] = start - lane_f
            en_t[y] = end - lane_f

    def gate_grads():
        for copy in local:
            copy.wait()
        gg = dot_nt(og_vm[...], proj_vm[...])
        ng = gg * gates_vm[...].astype(F32)
        for h in range(4):
            ngsrc[h] = ng[:, h * 128 : (h + 1) * 128]
        y_send(3, lambda h: ngsrc.at[h], ngbuf.at[yh])

    def pair(buf, y, at):
        return buf[y, pl.ds(at * 2, 2)].reshape(256, 128)

    def query_tiles(r):
        at = lax.rem(x - r + 4, 4)
        wrap = 1 - lax.div(x - r + 4, 4)
        for y in range(4):
            tiles = []
            for j in range(3 if r == 0 else 2):
                if y < j:
                    continue
                if r == 0:
                    ky, off = y - j, 0
                else:
                    ky, off = lax.rem(y - wrap - j + 4, 4), (wrap * FAR if y == j else 0)
                first = ((4 * ky + at) * 256 - off).astype(F32)
                tiles.append((r + 4 * j, ky, first))
            yield y, at, tiles

    def key_tiles(r):
        at = lax.rem(x + r, 4)
        wrap = lax.div(x + r, 4)
        for y in range(4):
            tiles = []
            for j in range(3 if r == 0 else 2):
                if y + j > 3:
                    continue
                if r == 0:
                    qy, off = y + j, 0
                else:
                    qy, off = lax.rem(y + wrap + j, 4), (wrap * FAR if y + j == 3 else 0)
                first = ((4 * qy + at) * 256 + off).astype(F32)
                tiles.append((r + 4 * j, qy, first))
            yield y, at, tiles

    def forward(r):
        for y, at, tiles in query_tiles(r):
            part = None if r == 0 else acc_m[y]
            for d, ky, first in tiles:
                s = dot_nt(qbuf[y, xc], pair(kbuf, ky, at))
                t = s * HALF_SCALE + bias_at(tab_q, d)
                t = jnp.where(st_t[y] <= first, t, NEG)
                w = (t * jnp.tanh(t) + t).astype(BF16)
                add = dot_nn(w, pair(vbuf, ky, at))
                part = add if part is None else part + add
            acc_m[y] = part

    def fold(ds):
        return jnp.sum(ds.reshape(16, 8, 256), axis=0)

    def query_grads(r):
        sums = {}
        for y, at, tiles in query_tiles(r):
            part = None if r == 0 else acc_q[y]
            for d, ky, first in tiles:
                keys = pair(kbuf, ky, at)
                s = dot_nt(qbuf[y, xc], keys)
                t = s * HALF_SCALE + bias_at(tab_q, d)
                t = jnp.where(st_t[y] <= first, t, NEG)
                th = jnp.tanh(t)
                ds = dot_nt(gbuf[y, xc], pair(vbuf, ky, at)) * ((1.0 + th) * (1.0 + t * (1.0 - th)))
                if d in TABLED:
                    slot = acc_bias.at[TABLED.index(d)]
                    slot[...] = ds if d not in sums else slot[...] + ds
                else:
                    slot = acc_far.at[(3, 5, 6, 7, 8).index(d)]
                    slot[...] = fold(ds) if d not in sums else slot[...] + fold(ds)
                sums[d] = True
                add = dot_nn(ds.astype(BF16), keys)
                part = add if part is None else part + add
            acc_q[y] = part

    def key_grads(r):
        for y, at, tiles in key_tiles(r):
            key_part = None if r == 0 else acc_k[y]
            value_part = None if r == 0 else acc_v[y]
            for d, qy, first in tiles:
                queries, grads = pair(qbuf, qy, at), pair(gbuf, qy, at)
                s = dot_nt(kbuf[y, xc], queries)
                t = s * HALF_SCALE + bias_at(tab_k, d)
                t = jnp.where(en_t[y] > first, t, NEG)
                th = jnp.tanh(t)
                one = 1.0 + th
                w = (t * one).astype(BF16)
                ds = dot_nt(vbuf[y, xc], grads) * (one * (1.0 + t * (1.0 - th)))
                add_k = dot_nn(ds.astype(BF16), queries)
                add_v = dot_nn(w, grads)
                key_part = add_k if key_part is None else key_part + add_k
                value_part = add_v if value_part is None else value_part + add_v
            acc_k[y] = key_part
            acc_v[y] = value_part

    def own_cols(h):
        return pl.ds(pl.multiple_of(h * 128, 128), 128)

    def give_back(a, src, out_ref):
        for y in range(4):
            send(
                src.at[y], out_ref.at[0, :, own_cols(yh)], ret_sems.at[a, yh], (odp, y * 8 + xc)
            )

    y_wait(0, lambda s: kbuf.at[s, xc])
    x_start(0, kbuf)
    gate_grads()
    y_wait(1, lambda s: vbuf.at[s, xc])
    x_start(1, vbuf)
    x_near(0, kbuf)
    build_tables()
    x_rest(0, kbuf)
    y_wait(2, lambda s: qbuf.at[s, xc])
    x_start(2, qbuf)
    x_near(1, vbuf)
    x_far(0, kbuf)
    build_bounds()
    sib_own(0, kbuf)
    sib_own(1, vbuf)
    forward(0)
    x_rest(1, vbuf)
    x_near(2, qbuf)
    x_far(1, vbuf)
    sib_near(0, kbuf)
    sib_near(1, vbuf)
    forward(LEFT)
    forward(RIGHT)
    x_rest(2, qbuf)
    sib_far(0, kbuf)
    sib_far(1, vbuf)
    forward(DIAG)
    x_far(2, qbuf)

    y_wait(3, lambda s: ngbuf.at[s])
    for y in range(4):
        mixed = acc_m[y]
        centred = mixed - jnp.mean(mixed, axis=1, keepdims=True)
        inverse = lax.rsqrt(jnp.mean(centred * centred, axis=1, keepdims=True) + EPS)
        normed = centred * inverse
        nrmsrc[y] = normed.astype(BF16)
        ng = ngbuf[y]
        grad = ng - jnp.mean(ng, axis=1, keepdims=True)
        grad = (grad - normed * jnp.mean(ng * normed, axis=1, keepdims=True)) * inverse
        gbuf[y, xc] = grad.astype(BF16)
    x_start(3, gbuf)
    for y in range(4):
        send(nrmsrc.at[y], nrmbuf.at[yh], ret_sems.at[0, yh], (odp, y * 8 + xc))

    query_grads(0)
    x_near(3, gbuf)
    query_grads(LEFT)
    x_rest(3, gbuf)
    x_far(3, gbuf)
    query_grads(RIGHT)
    query_grads(DIAG)
    for y in range(4):
        out_q[y] = (acc_q[y] * 0.5).astype(BF16)
    give_back(1, out_q, dq_ref)

    rows = []
    for b in range(12):
        parts = []
        for at, d in enumerate(TABLED):
            low, high = spans[d]
            if low <= b <= high:
                got = acc_bias[at]
                dist = dist_q + 256 * d
                if b > low:
                    got = jnp.where(dist >= 2 ** (b - 1), got, 0.0)
                if b < high:
                    got = jnp.where(dist < 2**b, got, 0.0)
                parts.append(fold(got))
        if b == 10:
            parts.append(acc_far[0])
        if b == 11:
            parts += [acc_far[at] for at in range(1, 5)]
        whole = parts[0]
        for part in parts[1:]:
            whole = whole + part
        folded = jnp.sum(whole, axis=0, keepdims=True)
        rows.append(folded[:, :128] + folded[:, 128:])
    rows.append(jnp.zeros((4, 128), F32))
    shares = jnp.concatenate(rows, axis=0) * 0.5

    def share_out(stage, me, mine):
        red[stage, me] = mine
        for k in range(1, 8):
            dev, other = partners[stage](k)
            send(red.at[stage, me], red.at[stage, me], red_sems.at[stage, me], dev)

    def take_in(stage):
        for k in range(1, 8):
            other = partners[stage](k)[1]
            arrived(red.at[stage, other], red_sems.at[stage, other])

    def sum_of(stage):
        total = red[stage, 0]
        for k in range(1, 8):
            total = total + red[stage, k]
        return total

    share_out(0, z, shares)
    sib_own(2, qbuf)
    sib_own(3, gbuf)
    key_grads(0)
    take_in(0)
    share_out(1, xc, sum_of(0))
    sib_near(2, qbuf)
    sib_near(3, gbuf)
    key_grads(LEFT)
    key_grads(RIGHT)
    take_in(1)
    share_out(2, yi, sum_of(1))
    sib_far(2, qbuf)
    sib_far(3, gbuf)
    key_grads(DIAG)
    for y in range(4):
        out_v[y] = acc_v[y].astype(BF16)
        out_k[y] = (acc_k[y] * 0.5).astype(BF16)
    give_back(3, out_v, dv_ref)
    give_back(2, out_k, dk_ref)

    for h in range(4):
        arrived(nrmbuf.at[h], ret_sems.at[0, h])
        cols = slice(h * 128, (h + 1) * 128)
        gated_vm[:, cols] = (nrmbuf[h].astype(F32) * gates_vm[:, cols].astype(F32)).astype(BF16)
    outproj_vm[...] = dot_nn(gated_vm[...], proj_vm[...]).astype(BF16)
    out_copy = pltpu.make_async_copy(outproj_vm, projected_ref.at[0], local_sems.at[3])
    out_copy.start()

    take_in(2)
    by_head = lax.broadcasted_iota(jnp.int32, (16, 128), 0)
    by_lane = lax.broadcasted_iota(jnp.int32, (16, 128), 1)
    for h in range(4):
        sums = jnp.sum(red[2, h] + red[2, 4 + h], axis=1, keepdims=True)
        spread = jnp.where(by_head == by_lane, jnp.broadcast_to(sums, (16, 128)), 0.0)
        bias_ref[h : h + 1, :] = jnp.sum(spread, axis=0, keepdims=True)[:, :16]

    for a, out_ref in ((1, dq_ref), (3, dv_ref), (2, dk_ref)):
        for h in range(4):
            arrived(out_ref.at[0, :, h * 128 : (h + 1) * 128], ret_sems.at[a, h])
    out_copy.wait()
    for copy in pending:
        copy.wait_send()


def shards(queries, keys, values, gates, out_proj, out_grad, lengths, rel_bias):
    anywhere = pl.BlockSpec(memory_space=pl.ANY)
    scalars = pl.BlockSpec(memory_space=pltpu.SMEM)
    whole = pl.BlockSpec(memory_space=pltpu.VMEM)
    shape = jax.ShapeDtypeStruct
    head_rows = pltpu.VMEM((4, 8, 128, 128), BF16)
    own_rows = pltpu.VMEM((4, 128, 128), BF16)
    own_sums = pltpu.VMEM((4, 128, 128), F32)
    tables = pltpu.VMEM((4, 128, 256), F32)
    dma = pltpu.SemaphoreType.DMA
    return pl.pallas_call(
        kernel,
        out_shape=(
            shape((1, 128, 1024), BF16),
            shape((1, 128, 512), BF16),
            shape((1, 128, 512), BF16),
            shape((1, 128, 512), BF16),
            shape((4, 16), F32),
        ),
        in_specs=[anywhere] * 6 + [scalars] * 2,
        out_specs=(anywhere, anywhere, anywhere, anywhere, whole),
        scratch_shapes=[
            head_rows, head_rows, head_rows, head_rows,
            own_sums, own_sums, own_rows, own_rows,
            pltpu.VMEM((8, 128), F32), pltpu.VMEM((8, 128), F32),
            pltpu.VMEM((128, 1024), BF16),
            pltpu.VMEM((128, 512), BF16),
            pltpu.VMEM((512, 1024), BF16),
            pltpu.VMEM((128, 512), BF16),
            pltpu.VMEM((128, 1024), BF16),
            tables, tables, tables, tables,
            own_sums, own_sums, own_sums, own_sums,
            own_rows, own_rows, own_rows,
            tables, pltpu.VMEM((5, 8, 256), F32),
            pltpu.VMEM((3, 8, 16, 128), F32),
            dma((112,)), dma((4, 4)), dma((4, 13)), dma((4, 4)), dma((3, 8)), dma((1,)), dma((4,)),
        ],
        compiler_params=pltpu.CompilerParams(
            collective_id=0, has_side_effects=True, vmem_limit_bytes=48 * 2**20
        ),
    )(queries, keys, values, gates, out_proj, out_grad, lengths, rel_bias)


def solution(mesh):
    rows = P("dp", "seq", None)
    return jax.shard_map(
        shards,
        mesh=mesh,
        in_specs=(rows, rows, rows, rows, P(), rows, P("dp", None), P()),
        out_specs=(rows, rows, rows, rows, P()),
        check_vma=False,
    )
```

```python
import jax
import jax.numpy as jnp
from jax import lax
from jax.experimental import pallas as pl
from jax.experimental.pallas import tpu as pltpu
from jax.sharding import PartitionSpec as P

F32 = jnp.float32
BF16 = jnp.bfloat16
EPS = 1e-05
NEG = -1e5
HALF_SCALE = 0.5 * 128 ** (-0.5)
FAR = 1 << 20
TABLED = (0, 1, 2, 4)
LEFT, DIAG, RIGHT = 1, 2, 3


def dot_nt(a, b):
    return lax.dot_general(a, b, (((1,), (1,)), ((), ())), preferred_element_type=F32)


def dot_nn(a, b):
    return jnp.dot(a, b, preferred_element_type=F32)


def kernel(
    q_in, k_in, v_in, gates_in, proj_in, og_in, len_in, rb_in,
    projected_ref, dq_ref, dk_ref, dv_ref, bias_ref,
    kbuf, vbuf, qbuf, gbuf, ngbuf, ngsrc, nrmsrc, nrmbuf, lensrc, lenbuf,
    og_vm, gates_vm, proj_vm, gated_vm, outproj_vm,
    slopes, tab_b, tab_q, tab_k, st_t, en_t, acc_m, acc_q, acc_k, acc_v,
    out_q, out_k, out_v, acc_bias, acc_far, red,
    len_ref, rb_ref,
    send_sems, y_sems, x_sems, ret_sems, red_sems, len_sem, local_sems,
):
    dp = lax.axis_index("dp")
    seq = lax.axis_index("seq")
    ylo, z = lax.div(dp, 8), lax.rem(dp, 8)
    yh, xc = lax.div(seq, 8), lax.rem(seq, 8)
    x, c = lax.div(xc, 2), lax.rem(xc, 2)
    odp = lax.rem(dp + 8, 16)
    yi = ylo * 4 + yh

    def place(rel):
        return lax.rem(x + rel, 4)

    left, right, diag = place(3), place(1), place(2)
    dev_left = (dp, yh * 8 + left * 2 + c)
    dev_right = (dp, yh * 8 + right * 2 + c)
    dev_sib = (dp, yh * 8 + x * 2 + 1 - c)

    def z_partner(k):
        other = lax.rem(z + k, 8)
        return (ylo * 8 + other, seq), other

    def xc_partner(k):
        other = lax.rem(xc + k, 8)
        return (dp, yh * 8 + other), other

    def y_partner(k):
        other = lax.rem(yi + k, 8)
        return (lax.div(other, 4) * 8 + z, lax.rem(other, 4) * 8 + xc), other

    partners = (y_partner, xc_partner, z_partner)

    barrier = pltpu.get_barrier_semaphore()

    def greet(dev):
        pl.semaphore_signal(barrier, inc=1, device_id=dev, device_id_type=pl.DeviceIdType.MESH)

    def group_of(plane):
        return plane - lax.div(plane, 4) * lax.rem(plane, 4)

    def greet_planes(same):
        for k in range(1, 8):
            dev, other = z_partner(k)
            meets = group_of(other) == group_of(z)
            pl.when(meets if same else jnp.logical_not(meets))(lambda dev=dev: greet(dev))

    for partner in (y_partner, xc_partner):
        for k in range(1, 8):
            greet(partner(k)[0])
    greet_planes(True)
    earlier = z + lax.div(z, 4) * (7 - z)

    local = [
        pltpu.make_async_copy(og_in.at[0], og_vm, local_sems.at[0]),
        pltpu.make_async_copy(proj_in, proj_vm, local_sems.at[1]),
        pltpu.make_async_copy(gates_in.at[0], gates_vm, local_sems.at[2]),
    ]
    small = [
        pltpu.make_async_copy(len_in, len_ref, local_sems.at[4]),
        pltpu.make_async_copy(rb_in, rb_ref, local_sems.at[5]),
    ]
    for copy in small + local:
        copy.start()

    pending = []

    def send(src, dst, recv_sem, dev):
        copy = pltpu.make_async_remote_copy(
            src_ref=src, dst_ref=dst, send_sem=send_sems.at[len(pending)], recv_sem=recv_sem,
            device_id=dev, device_id_type=pl.DeviceIdType.MESH,
        )
        copy.start()
        pending.append(copy)

    def arrived(dst, sem):
        pltpu.make_async_copy(dst, dst, sem).wait()

    pl.semaphore_wait(barrier, 14 + earlier)

    def y_send(a, src_of, dst):
        for h in range(4):
            send(src_of(h), dst, y_sems.at[a, yh], (odp, h * 8 + xc))

    def y_wait(a, dst_of):
        for s in range(4):
            arrived(dst_of(s), y_sems.at[a, s])

    for a, (src, buf) in enumerate(((k_in, kbuf), (v_in, vbuf), (q_in, qbuf))):
        y_send(a, lambda h, src=src: src.at[0, :, h * 128 : (h + 1) * 128], buf.at[yh, xc])
    greet_planes(False)
    for copy in small:
        copy.wait()
    ends = [len_ref[0, 0]]
    for u in range(1, 4):
        ends.append(ends[-1] + len_ref[0, u])
    row_at = lax.broadcasted_iota(jnp.int32, (8, 128), 0)
    end_rows = jnp.zeros((8, 128), F32)
    for u in range(4):
        end_rows = jnp.where(row_at == u, ends[u].astype(F32), end_rows)
    lensrc[...] = end_rows
    send(lensrc, lenbuf, len_sem.at[0], (odp, seq))

    def piece(buf, half, at):
        return buf.at[pl.ds(2 * half, 2), at]

    def own_of(at):
        return at * 2 + c

    def x_half(a, buf, half):
        part = piece(buf, half, own_of(x))
        if half == 0:
            send(part, part, x_sems.at[a, 0], dev_right)
            send(part, part, x_sems.at[a, 4], dev_left)
            send(part, part, x_sems.at[a, 6], dev_sib)
        else:
            send(part, part, x_sems.at[a, 3], dev_left)
            send(part, part, x_sems.at[a, 1], dev_right)
            send(part, part, x_sems.at[a, 13], dev_sib)

    def x_start(a, buf):
        x_half(a, buf, 0)
        x_half(a, buf, 1)

    def x_pass(a, buf, steps):
        for half, whose, slot, to in steps:
            part = piece(buf, half, own_of(whose))
            arrived(part, x_sems.at[a, slot])
            if to is not None:
                device, next_slot = to
                send(part, part, x_sems.at[a, next_slot], device)
            send(part, part, x_sems.at[a, slot + 7], dev_sib)

    def x_near(a, buf):
        x_pass(a, buf, ((0, left, 0, (dev_right, 2)), (1, right, 3, (dev_left, 5))))

    def x_rest(a, buf):
        x_pass(a, buf, ((1, left, 1, None), (0, right, 4, None)))

    def x_far(a, buf):
        x_pass(a, buf, ((0, diag, 2, None), (1, diag, 5, None)))

    def sib_of(at):
        return at * 2 + 1 - c

    def sib_own(a, buf):
        arrived(piece(buf, 0, sib_of(x)), x_sems.at[a, 6])
        arrived(piece(buf, 1, sib_of(x)), x_sems.at[a, 13])

    def sib_near(a, buf):
        arrived(piece(buf, 0, sib_of(left)), x_sems.at[a, 7])
        arrived(piece(buf, 1, sib_of(right)), x_sems.at[a, 10])
        arrived(piece(buf, 1, sib_of(left)), x_sems.at[a, 8])
        arrived(piece(buf, 0, sib_of(right)), x_sems.at[a, 11])

    def sib_far(a, buf):
        arrived(piece(buf, 0, sib_of(diag)), x_sems.at[a, 9])
        arrived(piece(buf, 1, sib_of(diag)), x_sems.at[a, 12])

    wide = (128, 256)
    sub = lax.broadcasted_iota(jnp.int32, wide, 0)
    lane = lax.broadcasted_iota(jnp.int32, wide, 1)
    dist_q = 128 * c + sub - lane
    dist_k = lane - sub - 128 * c
    half_bias = [0.5 * rb_ref[yh, b] for b in range(12)]

    def biases(dist, low, high, values):
        filled = jnp.full(wide, values[low], F32)
        for b in range(low + 1, high + 1):
            filled = jnp.where(dist >= 2 ** (b - 1), values[b], filled)
        return filled

    spans = {0: (0, 9), 1: (1, 9), 2: (9, 10), 4: (10, 11)}

    def build_tables():
        for tab, dist in ((tab_q, dist_q), (tab_k, dist_k)):
            for at, d in enumerate(TABLED):
                filled = biases(dist + 256 * d, *spans[d], half_bias)
                if d == 0:
                    filled = jnp.where(dist >= 0, filled, NEG)
                tab[at] = filled
        for at, d in enumerate(TABLED):
            tab_b[at] = biases(dist_q + 256 * d, *spans[d], [float(b) for b in range(12)])

    def bias_at(tab, d):
        if d in TABLED:
            return tab[TABLED.index(d)]
        return half_bias[10 if d == 3 else 11]

    def build_bounds():
        arrived(lenbuf, len_sem.at[0])
        sub_f, lane_f = sub.astype(F32), lane.astype(F32)
        ends_at = [jnp.broadcast_to(lenbuf[u : u + 1, 0:1], wide) for u in range(4)]
        for y in range(4):
            pos = sub_f + ((8 * y + xc) * 128).astype(F32)
            start = jnp.zeros(wide, F32)
            end = ends_at[3]
            for u in (0, 1, 2):
                start = jnp.where(pos >= ends_at[u], ends_at[u], start)
            for u in (2, 1, 0):
                end = jnp.where(pos < ends_at[u], ends_at[u], end)
            st_t[y] = start - lane_f
            en_t[y] = end - lane_f

    def gate_grads():
        for copy in local:
            copy.wait()
        gg = dot_nt(og_vm[...], proj_vm[...])
        ng = gg * gates_vm[...].astype(F32)
        for h in range(4):
            ngsrc[h] = ng[:, h * 128 : (h + 1) * 128]
        y_send(3, lambda h: ngsrc.at[h], ngbuf.at[yh])

    def pair(buf, y, at):
        return buf[y, pl.ds(at * 2, 2)].reshape(256, 128)

    def query_tiles(r, ys):
        at = lax.rem(x - r + 4, 4)
        wrap = 1 - lax.div(x - r + 4, 4)
        for y in ys:
            tiles = []
            for j in range(3 if r == 0 else 2):
                if y < j:
                    continue
                if r == 0:
                    ky, off = y - j, 0
                else:
                    ky, off = lax.rem(y - wrap - j + 4, 4), (wrap * FAR if y == j else 0)
                first = ((4 * ky + at) * 256 - off).astype(F32)
                tiles.append((r + 4 * j, ky, first))
            yield y, at, tiles

    def key_tiles(r, ys):
        at = lax.rem(x + r, 4)
        wrap = lax.div(x + r, 4)
        for y in ys:
            tiles = []
            for j in range(3 if r == 0 else 2):
                if y + j > 3:
                    continue
                if r == 0:
                    qy, off = y + j, 0
                else:
                    qy, off = lax.rem(y + wrap + j, 4), (wrap * FAR if y + j == 3 else 0)
                first = ((4 * qy + at) * 256 + off).astype(F32)
                tiles.append((r + 4 * j, qy, first))
            yield y, at, tiles

    def slot_of(y, d):
        return (0, 4, 12, 21)[y] + d

    def forward(r, ys=range(4)):
        for y, at, tiles in query_tiles(r, ys):
            part = None if r == 0 else acc_m[y]
            for d, ky, first in tiles:
                s = dot_nt(qbuf[y, xc], pair(kbuf, ky, at))
                t = s * HALF_SCALE + bias_at(tab_q, d)
                t = jnp.where(st_t[y] <= first, t, NEG)
                th = jnp.tanh(t)
                one = 1.0 + th
                slopes[slot_of(y, d)] = one * (1.0 + t * (1.0 - th))
                add = dot_nn((t * one).astype(BF16), pair(vbuf, ky, at))
                part = add if part is None else part + add
            acc_m[y] = part

    def fold(ds):
        return jnp.sum(ds.reshape(16, 8, 256), axis=0)

    def query_grads(r, ys=range(4)):
        sums = {}
        for y, at, tiles in query_tiles(r, ys):
            part = None if r == 0 else acc_q[y]
            for d, ky, first in tiles:
                keys = pair(kbuf, ky, at)
                ds = dot_nt(gbuf[y, xc], pair(vbuf, ky, at)) * slopes[slot_of(y, d)]
                if d in TABLED:
                    slot = acc_bias.at[TABLED.index(d)]
                    slot[...] = ds if d not in sums else slot[...] + ds
                else:
                    slot = acc_far.at[(3, 5, 6, 7, 8).index(d)]
                    slot[...] = fold(ds) if d not in sums else slot[...] + fold(ds)
                sums[d] = True
                add = dot_nn(ds.astype(BF16), keys)
                part = add if part is None else part + add
            acc_q[y] = part

    def key_grads(r, ys=range(4)):
        for y, at, tiles in key_tiles(r, ys):
            key_part = None if r == 0 else acc_k[y]
            value_part = None if r == 0 else acc_v[y]
            for d, qy, first in tiles:
                queries, grads = pair(qbuf, qy, at), pair(gbuf, qy, at)
                s = dot_nt(kbuf[y, xc], queries)
                t = s * HALF_SCALE + bias_at(tab_k, d)
                t = jnp.where(en_t[y] > first, t, NEG)
                th = jnp.tanh(t)
                one = 1.0 + th
                w = (t * one).astype(BF16)
                ds = dot_nt(vbuf[y, xc], grads) * (one * (1.0 + t * (1.0 - th)))
                add_k = dot_nn(ds.astype(BF16), queries)
                add_v = dot_nn(w, grads)
                key_part = add_k if key_part is None else key_part + add_k
                value_part = add_v if value_part is None else value_part + add_v
            acc_k[y] = key_part
            acc_v[y] = value_part

    def own_cols(h):
        return pl.ds(pl.multiple_of(h * 128, 128), 128)

    def give_back(a, src, out_ref, ys=range(4)):
        for y in ys:
            send(
                src.at[y], out_ref.at[0, :, own_cols(yh)], ret_sems.at[a, yh], (odp, y * 8 + xc)
            )

    y_wait(0, lambda s: kbuf.at[s, xc])
    x_start(0, kbuf)
    gate_grads()
    y_wait(1, lambda s: vbuf.at[s, xc])
    x_start(1, vbuf)
    build_tables()
    x_near(0, kbuf)
    x_rest(0, kbuf)
    y_wait(2, lambda s: qbuf.at[s, xc])
    build_bounds()
    x_near(1, vbuf)
    x_start(2, qbuf)
    sib_own(0, kbuf)
    sib_own(1, vbuf)
    forward(0)
    x_far(0, kbuf)
    x_rest(1, vbuf)
    sib_near(0, kbuf)
    sib_near(1, vbuf)
    forward(LEFT)
    x_far(1, vbuf)
    x_near(2, qbuf)
    forward(RIGHT)
    x_rest(2, qbuf)
    sib_far(0, kbuf)
    sib_far(1, vbuf)
    y_wait(3, lambda s: ngbuf.at[s])

    def finish(y):
        mixed = acc_m[y]
        centred = mixed - jnp.mean(mixed, axis=1, keepdims=True)
        inverse = lax.rsqrt(jnp.mean(centred * centred, axis=1, keepdims=True) + EPS)
        normed = centred * inverse
        nrmsrc[y] = normed.astype(BF16)
        ng = ngbuf[y]
        grad = ng - jnp.mean(ng, axis=1, keepdims=True)
        grad = (grad - normed * jnp.mean(ng * normed, axis=1, keepdims=True)) * inverse
        gbuf[y, xc] = grad.astype(BF16)

    for half in range(2):
        ys = (2 * half, 2 * half + 1)
        forward(DIAG, ys)
        for y in ys:
            finish(y)
        x_half(3, gbuf, half)
    for y in range(4):
        send(nrmsrc.at[y], nrmbuf.at[yh], ret_sems.at[0, yh], (odp, y * 8 + xc))
    x_far(2, qbuf)

    query_grads(0)
    query_grads(LEFT)
    query_grads(RIGHT)
    x_near(3, gbuf)
    query_grads(DIAG)
    rows = []
    for b in range(12):
        parts = []
        for at, d in enumerate(TABLED):
            low, high = spans[d]
            if low <= b <= high:
                parts.append(fold(jnp.where(tab_b[at] == float(b), acc_bias[at], 0.0)))
        if b == 10:
            parts.append(acc_far[0])
        if b == 11:
            parts += [acc_far[at] for at in range(1, 5)]
        whole = parts[0]
        for part in parts[1:]:
            whole = whole + part
        folded = jnp.sum(whole, axis=0, keepdims=True)
        rows.append(folded[:, :128] + folded[:, 128:])
    rows.append(jnp.zeros((4, 128), F32))
    shares = jnp.concatenate(rows, axis=0) * 0.5

    def share_out(stage, me, mine):
        red[stage, me] = mine
        for k in range(1, 8):
            dev, other = partners[stage](k)
            send(red.at[stage, me], red.at[stage, me], red_sems.at[stage, me], dev)

    def take_in(stage):
        for k in range(1, 8):
            other = partners[stage](k)[1]
            arrived(red.at[stage, other], red_sems.at[stage, other])

    def sum_of(stage):
        total = red[stage, 0]
        for k in range(1, 8):
            total = total + red[stage, k]
        return total

    by_head = lax.broadcasted_iota(jnp.int32, (16, 128), 0)
    by_lane = lax.broadcasted_iota(jnp.int32, (16, 128), 1)

    def heads_side_by_side():
        packed = jnp.zeros((16, 128), F32)
        for h in range(4):
            sums = jnp.sum(red[0, h] + red[0, 4 + h], axis=1, keepdims=True)
            packed = jnp.where(by_lane == h, jnp.broadcast_to(sums, (16, 128)), packed)
        return packed

    pl.when(z < 4)(lambda: pl.semaphore_wait(barrier, 7 - earlier))
    share_out(0, yi, shares)
    x_rest(3, gbuf)
    for y in range(4):
        out_q[y] = (acc_q[y] * 0.5).astype(BF16)
    give_back(1, out_q, dq_ref)
    sib_own(2, qbuf)
    sib_own(3, gbuf)
    key_grads(0)
    x_far(3, gbuf)
    take_in(0)
    share_out(1, xc, heads_side_by_side())
    sib_near(2, qbuf)
    sib_near(3, gbuf)
    key_grads(LEFT)
    take_in(1)
    share_out(2, z, sum_of(1))
    key_grads(RIGHT)
    sib_far(2, qbuf)
    sib_far(3, gbuf)
    for half in range(2):
        ys = (2 * half, 2 * half + 1)
        key_grads(DIAG, ys)
        for y in ys:
            out_v[y] = acc_v[y].astype(BF16)
            out_k[y] = (acc_k[y] * 0.5).astype(BF16)
        give_back(3, out_v, dv_ref, ys)
        give_back(2, out_k, dk_ref, ys)

    for h in range(4):
        arrived(nrmbuf.at[h], ret_sems.at[0, h])
        cols = slice(h * 128, (h + 1) * 128)
        gated_vm[:, cols] = (nrmbuf[h].astype(F32) * gates_vm[:, cols].astype(F32)).astype(BF16)
    outproj_vm[...] = dot_nn(gated_vm[...], proj_vm[...]).astype(BF16)
    out_copy = pltpu.make_async_copy(outproj_vm, projected_ref.at[0], local_sems.at[3])
    out_copy.start()

    take_in(2)
    heads = sum_of(2)
    for h in range(4):
        sums = jnp.sum(jnp.where(by_lane == h, heads, 0.0), axis=1, keepdims=True)
        spread = jnp.where(by_head == by_lane, jnp.broadcast_to(sums, (16, 128)), 0.0)
        bias_ref[h : h + 1, :] = jnp.sum(spread, axis=0, keepdims=True)[:, :16]

    for a, out_ref in ((1, dq_ref), (3, dv_ref), (2, dk_ref)):
        for h in range(4):
            arrived(out_ref.at[0, :, h * 128 : (h + 1) * 128], ret_sems.at[a, h])
    out_copy.wait()
    for copy in pending:
        copy.wait_send()


def hand_out(*refs):
    for i in range(5):
        refs[5 + i][...] = refs[i][...]


def shards(queries, keys, values, gates, out_proj, out_grad, lengths, rel_bias):
    anywhere = pl.BlockSpec(memory_space=pl.ANY)
    whole = pl.BlockSpec(memory_space=pltpu.VMEM)
    shape = jax.ShapeDtypeStruct
    head_rows = pltpu.VMEM((4, 8, 128, 128), BF16)
    own_rows = pltpu.VMEM((4, 128, 128), BF16)
    own_sums = pltpu.VMEM((4, 128, 128), F32)
    tables = pltpu.VMEM((4, 128, 256), F32)
    dma = pltpu.SemaphoreType.DMA
    made = (
            shape((1, 128, 1024), BF16),
            shape((1, 128, 512), BF16),
            shape((1, 128, 512), BF16),
            shape((1, 128, 512), BF16),
            shape((4, 16), F32),
        )
    results = pl.pallas_call(
        kernel,
        out_shape=made,
        in_specs=[anywhere] * 8,
        out_specs=(anywhere, anywhere, anywhere, anywhere, whole),
        scratch_shapes=[
            head_rows, head_rows, head_rows, head_rows,
            own_sums, own_sums, own_rows, own_rows,
            pltpu.VMEM((8, 128), F32), pltpu.VMEM((8, 128), F32),
            pltpu.VMEM((128, 1024), BF16),
            pltpu.VMEM((128, 512), BF16),
            pltpu.VMEM((512, 1024), BF16),
            pltpu.VMEM((128, 512), BF16),
            pltpu.VMEM((128, 1024), BF16),
            pltpu.VMEM((30, 128, 256), F32), pltpu.VMEM((4, 128, 256), F32),
            tables, tables, tables, tables,
            own_sums, own_sums, own_sums, own_sums,
            own_rows, own_rows, own_rows,
            tables, pltpu.VMEM((5, 8, 256), F32),
            pltpu.VMEM((3, 8, 16, 128), F32),
            pltpu.SMEM((1, 4), jnp.int32), pltpu.SMEM((4, 16), F32),
            dma((116,)), dma((4, 4)), dma((4, 14)), dma((4, 4)), dma((3, 8)), dma((1,)), dma((6,)),
        ],
        compiler_params=pltpu.CompilerParams(
            collective_id=0, has_side_effects=True, vmem_limit_bytes=60 * 2**20
        ),
    )(queries, keys, values, gates, out_proj, out_grad, lengths, rel_bias)
    return pl.pallas_call(
        hand_out,
        out_shape=made,
        in_specs=[whole] * 5,
        out_specs=(whole,) * 5,
    )(*results)


def solution(mesh):
    rows = P("dp", "seq", None)
    return jax.shard_map(
        shards,
        mesh=mesh,
        in_specs=(rows, rows, rows, rows, P(), rows, P("dp", None), P()),
        out_specs=(rows, rows, rows, rows, P()),
        check_vma=False,
    )
```

```python
import jax
import jax.numpy as jnp
from jax import lax
from jax.experimental import pallas as pl
from jax.experimental.pallas import tpu as pltpu
from jax.sharding import PartitionSpec as P

F32 = jnp.float32
BF16 = jnp.bfloat16
EPS = 1e-05
NEG = -1e5
HALF_SCALE = 0.5 * 128 ** (-0.5)
FAR = 1 << 20
TABLED = (0, 1, 2, 4)
LEFT, DIAG, RIGHT = 1, 2, 3


def dot_nt(a, b):
    return lax.dot_general(a, b, (((1,), (1,)), ((), ())), preferred_element_type=F32)


def dot_nn(a, b):
    return jnp.dot(a, b, preferred_element_type=F32)


def kernel(
    q_in, k_in, v_in, gates_in, proj_in, og_in, len_in, rb_in,
    projected_ref, dq_ref, dk_ref, dv_ref, bias_ref,
    kbuf, vbuf, qbuf, gbuf, ngbuf, ngsrc, nrmsrc, nrmbuf, lensrc, lenbuf,
    og_vm, gates_vm, proj_vm, gated_vm, outproj_vm,
    slopes, tab_b, tab_q, tab_k, st_t, en_t, acc_m, acc_q, acc_k, acc_v,
    out_q, out_k, out_v, acc_bias, acc_far, red,
    len_ref, rb_ref,
    send_sems, y_sems, x_sems, ret_sems, red_sems, len_sem, local_sems,
):
    dp = lax.axis_index("dp")
    seq = lax.axis_index("seq")
    ylo, z = lax.div(dp, 8), lax.rem(dp, 8)
    yh, xc = lax.div(seq, 8), lax.rem(seq, 8)
    x, c = lax.div(xc, 2), lax.rem(xc, 2)
    odp = lax.rem(dp + 8, 16)
    yi = ylo * 4 + yh

    def place(rel):
        return lax.rem(x + rel, 4)

    left, right, diag = place(3), place(1), place(2)
    dev_left = (dp, yh * 8 + left * 2 + c)
    dev_right = (dp, yh * 8 + right * 2 + c)
    dev_sib = (dp, yh * 8 + x * 2 + 1 - c)

    def z_partner(k):
        other = lax.rem(z + k, 8)
        return (ylo * 8 + other, seq), other

    def xc_partner(k):
        other = lax.rem(xc + k, 8)
        return (dp, yh * 8 + other), other

    def y_partner(k):
        other = lax.rem(yi + k, 8)
        return (lax.div(other, 4) * 8 + z, lax.rem(other, 4) * 8 + xc), other

    partners = (y_partner, xc_partner, z_partner)

    barrier = pltpu.get_barrier_semaphore()

    def greet(dev):
        pl.semaphore_signal(barrier, inc=1, device_id=dev, device_id_type=pl.DeviceIdType.MESH)

    def group_of(plane):
        return plane - lax.div(plane, 4) * lax.rem(plane, 4)

    def greet_planes(same):
        for k in range(1, 8):
            dev, other = z_partner(k)
            meets = group_of(other) == group_of(z)
            pl.when(meets if same else jnp.logical_not(meets))(lambda dev=dev: greet(dev))

    for partner in (y_partner, xc_partner):
        for k in range(1, 8):
            greet(partner(k)[0])
    greet_planes(True)
    earlier = z + lax.div(z, 4) * (7 - z)

    local = [
        pltpu.make_async_copy(og_in.at[0], og_vm, local_sems.at[0]),
        pltpu.make_async_copy(proj_in, proj_vm, local_sems.at[1]),
        pltpu.make_async_copy(gates_in.at[0], gates_vm, local_sems.at[2]),
    ]
    small = [
        pltpu.make_async_copy(len_in, len_ref, local_sems.at[4]),
        pltpu.make_async_copy(rb_in, rb_ref, local_sems.at[5]),
    ]
    for copy in small + local:
        copy.start()

    pending = []

    def send(src, dst, recv_sem, dev):
        copy = pltpu.make_async_remote_copy(
            src_ref=src, dst_ref=dst, send_sem=send_sems.at[len(pending)], recv_sem=recv_sem,
            device_id=dev, device_id_type=pl.DeviceIdType.MESH,
        )
        copy.start()
        pending.append(copy)

    def arrived(dst, sem):
        pltpu.make_async_copy(dst, dst, sem).wait()

    pl.semaphore_wait(barrier, 14 + earlier)

    def y_send(a, src_of, dst):
        for h in range(4):
            send(src_of(h), dst, y_sems.at[a, yh], (odp, h * 8 + xc))

    def y_wait(a, dst_of):
        for s in range(4):
            arrived(dst_of(s), y_sems.at[a, s])

    for a, (src, buf) in enumerate(((k_in, kbuf), (v_in, vbuf), (q_in, qbuf))):
        y_send(a, lambda h, src=src: src.at[0, :, h * 128 : (h + 1) * 128], buf.at[yh, xc])
    greet_planes(False)
    for copy in small:
        copy.wait()
    ends = [len_ref[0, 0]]
    for u in range(1, 4):
        ends.append(ends[-1] + len_ref[0, u])
    row_at = lax.broadcasted_iota(jnp.int32, (8, 128), 0)
    end_rows = jnp.zeros((8, 128), F32)
    for u in range(4):
        end_rows = jnp.where(row_at == u, ends[u].astype(F32), end_rows)
    lensrc[...] = end_rows
    send(lensrc, lenbuf, len_sem.at[0], (odp, seq))

    def piece(buf, half, at):
        return buf.at[pl.ds(2 * half, 2), at]

    def own_of(at):
        return at * 2 + c

    def x_half(a, buf, half):
        part = piece(buf, half, own_of(x))
        if half == 0:
            send(part, part, x_sems.at[a, 0], dev_right)
            send(part, part, x_sems.at[a, 4], dev_left)
            send(part, part, x_sems.at[a, 6], dev_sib)
        else:
            send(part, part, x_sems.at[a, 3], dev_left)
            send(part, part, x_sems.at[a, 1], dev_right)
            send(part, part, x_sems.at[a, 13], dev_sib)

    def x_start(a, buf):
        x_half(a, buf, 0)
        x_half(a, buf, 1)

    def x_pass(a, buf, steps):
        for half, whose, slot, to in steps:
            part = piece(buf, half, own_of(whose))
            arrived(part, x_sems.at[a, slot])
            if to is not None:
                device, next_slot = to
                send(part, part, x_sems.at[a, next_slot], device)
            send(part, part, x_sems.at[a, slot + 7], dev_sib)

    def x_near(a, buf):
        x_pass(a, buf, ((0, left, 0, (dev_right, 2)), (1, right, 3, (dev_left, 5))))

    def x_rest(a, buf):
        x_pass(a, buf, ((1, left, 1, None), (0, right, 4, None)))

    def x_far(a, buf):
        x_pass(a, buf, ((0, diag, 2, None), (1, diag, 5, None)))

    def sib_of(at):
        return at * 2 + 1 - c

    def sib_own(a, buf):
        arrived(piece(buf, 0, sib_of(x)), x_sems.at[a, 6])
        arrived(piece(buf, 1, sib_of(x)), x_sems.at[a, 13])

    def sib_near(a, buf):
        arrived(piece(buf, 0, sib_of(left)), x_sems.at[a, 7])
        arrived(piece(buf, 1, sib_of(right)), x_sems.at[a, 10])
        arrived(piece(buf, 1, sib_of(left)), x_sems.at[a, 8])
        arrived(piece(buf, 0, sib_of(right)), x_sems.at[a, 11])

    def sib_far(a, buf):
        arrived(piece(buf, 0, sib_of(diag)), x_sems.at[a, 9])
        arrived(piece(buf, 1, sib_of(diag)), x_sems.at[a, 12])

    wide = (128, 256)
    sub = lax.broadcasted_iota(jnp.int32, wide, 0)
    lane = lax.broadcasted_iota(jnp.int32, wide, 1)
    dist_q = 128 * c + sub - lane
    dist_k = lane - sub - 128 * c
    half_bias = [0.5 * rb_ref[yh, b] for b in range(12)]

    def biases(dist, low, high, values):
        filled = jnp.full(wide, values[low], F32)
        for b in range(low + 1, high + 1):
            filled = jnp.where(dist >= 2 ** (b - 1), values[b], filled)
        return filled

    spans = {0: (0, 9), 1: (1, 9), 2: (9, 10), 4: (10, 11)}

    def build_tables():
        for tab, dist in ((tab_q, dist_q), (tab_k, dist_k)):
            for at, d in enumerate(TABLED):
                filled = biases(dist + 256 * d, *spans[d], half_bias)
                if d == 0:
                    filled = jnp.where(dist >= 0, filled, NEG)
                tab[at] = filled
        for at, d in enumerate(TABLED):
            tab_b[at] = biases(dist_q + 256 * d, *spans[d], [float(b) for b in range(12)])

    def bias_at(tab, d):
        if d in TABLED:
            return tab[TABLED.index(d)]
        return half_bias[10 if d == 3 else 11]

    def build_bounds():
        arrived(lenbuf, len_sem.at[0])
        sub_f, lane_f = sub.astype(F32), lane.astype(F32)
        ends_at = [jnp.broadcast_to(lenbuf[u : u + 1, 0:1], wide) for u in range(4)]
        for y in range(4):
            pos = sub_f + ((8 * y + xc) * 128).astype(F32)
            start = jnp.zeros(wide, F32)
            end = ends_at[3]
            for u in (0, 1, 2):
                start = jnp.where(pos >= ends_at[u], ends_at[u], start)
            for u in (2, 1, 0):
                end = jnp.where(pos < ends_at[u], ends_at[u], end)
            st_t[y] = start - lane_f
            en_t[y] = end - lane_f

    def gate_grads():
        for copy in local:
            copy.wait()
        gg = dot_nt(og_vm[...], proj_vm[...])
        ng = gg * gates_vm[...].astype(F32)
        for h in range(4):
            ngsrc[h] = ng[:, h * 128 : (h + 1) * 128]
        y_send(3, lambda h: ngsrc.at[h], ngbuf.at[yh])

    def pair(buf, y, at):
        return buf[y, pl.ds(at * 2, 2)].reshape(256, 128)

    def query_tiles(r, ys):
        at = lax.rem(x - r + 4, 4)
        wrap = 1 - lax.div(x - r + 4, 4)
        for y in ys:
            tiles = []
            for j in range(3 if r == 0 else 2):
                if y < j:
                    continue
                if r == 0:
                    ky, off = y - j, 0
                else:
                    ky, off = lax.rem(y - wrap - j + 4, 4), (wrap * FAR if y == j else 0)
                first = ((4 * ky + at) * 256 - off).astype(F32)
                tiles.append((r + 4 * j, ky, first))
            yield y, at, tiles

    def key_tiles(r, ys):
        at = lax.rem(x + r, 4)
        wrap = lax.div(x + r, 4)
        for y in ys:
            tiles = []
            for j in range(3 if r == 0 else 2):
                if y + j > 3:
                    continue
                if r == 0:
                    qy, off = y + j, 0
                else:
                    qy, off = lax.rem(y + wrap + j, 4), (wrap * FAR if y + j == 3 else 0)
                first = ((4 * qy + at) * 256 + off).astype(F32)
                tiles.append((r + 4 * j, qy, first))
            yield y, at, tiles

    def slot_of(y, d):
        return (0, 4, 12, 21)[y] + d

    def forward(r, ys=range(4)):
        for y, at, tiles in query_tiles(r, ys):
            part = None if r == 0 else acc_m[y]
            for d, ky, first in tiles:
                s = dot_nt(qbuf[y, xc], pair(kbuf, ky, at))
                t = s * HALF_SCALE + bias_at(tab_q, d)
                t = jnp.where(st_t[y] <= first, t, NEG)
                th = jnp.tanh(t)
                one = 1.0 + th
                slopes[slot_of(y, d)] = one * (1.0 + t * (1.0 - th))
                add = dot_nn((t * one).astype(BF16), pair(vbuf, ky, at))
                part = add if part is None else part + add
            acc_m[y] = part

    def fold(ds):
        return jnp.sum(ds.reshape(16, 8, 256), axis=0)

    def query_grads(r, ys=range(4)):
        sums = {}
        for y, at, tiles in query_tiles(r, ys):
            part = None if r == 0 else acc_q[y]
            for d, ky, first in tiles:
                keys = pair(kbuf, ky, at)
                ds = dot_nt(gbuf[y, xc], pair(vbuf, ky, at)) * slopes[slot_of(y, d)]
                if d in TABLED:
                    slot = acc_bias.at[TABLED.index(d)]
                    slot[...] = ds if d not in sums else slot[...] + ds
                else:
                    slot = acc_far.at[(3, 5, 6, 7, 8).index(d)]
                    slot[...] = fold(ds) if d not in sums else slot[...] + fold(ds)
                sums[d] = True
                add = dot_nn(ds.astype(BF16), keys)
                part = add if part is None else part + add
            acc_q[y] = part

    def key_grads(r, ys=range(4)):
        for y, at, tiles in key_tiles(r, ys):
            key_part = None if r == 0 else acc_k[y]
            value_part = None if r == 0 else acc_v[y]
            for d, qy, first in tiles:
                queries, grads = pair(qbuf, qy, at), pair(gbuf, qy, at)
                s = dot_nt(kbuf[y, xc], queries)
                t = s * HALF_SCALE + bias_at(tab_k, d)
                t = jnp.where(en_t[y] > first, t, NEG)
                th = jnp.tanh(t)
                one = 1.0 + th
                w = (t * one).astype(BF16)
                ds = dot_nt(vbuf[y, xc], grads) * (one * (1.0 + t * (1.0 - th)))
                add_k = dot_nn(ds.astype(BF16), queries)
                add_v = dot_nn(w, grads)
                key_part = add_k if key_part is None else key_part + add_k
                value_part = add_v if value_part is None else value_part + add_v
            acc_k[y] = key_part
            acc_v[y] = value_part

    def own_cols(h):
        return pl.ds(pl.multiple_of(h * 128, 128), 128)

    def give_back(a, src, out_ref, ys=range(4)):
        for y in ys:
            send(
                src.at[y], out_ref.at[0, :, own_cols(yh)], ret_sems.at[a, yh], (odp, y * 8 + xc)
            )

    y_wait(0, lambda s: kbuf.at[s, xc])
    x_start(0, kbuf)
    gate_grads()
    y_wait(1, lambda s: vbuf.at[s, xc])
    x_start(1, vbuf)
    build_tables()
    x_near(0, kbuf)
    x_rest(0, kbuf)
    y_wait(2, lambda s: qbuf.at[s, xc])
    build_bounds()
    x_near(1, vbuf)
    x_start(2, qbuf)
    sib_own(0, kbuf)
    sib_own(1, vbuf)
    forward(0)
    x_far(0, kbuf)
    x_rest(1, vbuf)
    sib_near(0, kbuf)
    sib_near(1, vbuf)
    forward(LEFT)
    x_far(1, vbuf)
    x_near(2, qbuf)
    forward(RIGHT)
    x_rest(2, qbuf)
    sib_far(0, kbuf)
    sib_far(1, vbuf)
    y_wait(3, lambda s: ngbuf.at[s])

    def finish(y):
        mixed = acc_m[y]
        centred = mixed - jnp.mean(mixed, axis=1, keepdims=True)
        inverse = lax.rsqrt(jnp.mean(centred * centred, axis=1, keepdims=True) + EPS)
        normed = centred * inverse
        nrmsrc[y] = normed.astype(BF16)
        ng = ngbuf[y]
        grad = ng - jnp.mean(ng, axis=1, keepdims=True)
        grad = (grad - normed * jnp.mean(ng * normed, axis=1, keepdims=True)) * inverse
        gbuf[y, xc] = grad.astype(BF16)

    for half in range(2):
        ys = (2 * half, 2 * half + 1)
        forward(DIAG, ys)
        for y in ys:
            finish(y)
        x_half(3, gbuf, half)
    for y in range(4):
        send(nrmsrc.at[y], nrmbuf.at[yh], ret_sems.at[0, yh], (odp, y * 8 + xc))
    x_far(2, qbuf)

    query_grads(0)
    query_grads(LEFT)
    query_grads(RIGHT)
    x_near(3, gbuf)
    query_grads(DIAG)
    rows = []
    for b in range(12):
        parts = []
        for at, d in enumerate(TABLED):
            low, high = spans[d]
            if low <= b <= high:
                parts.append(fold(jnp.where(tab_b[at] == float(b), acc_bias[at], 0.0)))
        if b == 10:
            parts.append(acc_far[0])
        if b == 11:
            parts += [acc_far[at] for at in range(1, 5)]
        whole = parts[0]
        for part in parts[1:]:
            whole = whole + part
        folded = jnp.sum(whole, axis=0, keepdims=True)
        rows.append(folded[:, :128] + folded[:, 128:])
    rows.append(jnp.zeros((4, 128), F32))
    shares = jnp.sum(jnp.concatenate(rows, axis=0), axis=1, keepdims=True) * 0.5
    by_bucket = lax.broadcasted_iota(jnp.int32, (16, 128), 0)
    by_lane = lax.broadcasted_iota(jnp.int32, (16, 128), 1)
    shares = jnp.where(by_lane == by_bucket + 16 * yh, jnp.broadcast_to(shares, (16, 128)), 0.0)
    shares = jnp.sum(shares, axis=0, keepdims=True)

    def share_out(stage, me, mine):
        red[stage, me] = mine
        for k in range(1, 8):
            dev, other = partners[stage](k)
            send(red.at[stage, me], red.at[stage, me], red_sems.at[stage, me], dev)

    def take_in(stage):
        for k in range(1, 8):
            other = partners[stage](k)[1]
            arrived(red.at[stage, other], red_sems.at[stage, other])

    def sum_of(stage):
        total = red[stage, 0]
        for k in range(1, 8):
            total = total + red[stage, k]
        return total

    pl.when(z < 4)(lambda: pl.semaphore_wait(barrier, 7 - earlier))
    share_out(0, yi, shares)
    x_rest(3, gbuf)
    for y in range(4):
        out_q[y] = (acc_q[y] * 0.5).astype(BF16)
    give_back(1, out_q, dq_ref)
    sib_own(2, qbuf)
    sib_own(3, gbuf)
    key_grads(0)
    x_far(3, gbuf)
    sib_near(2, qbuf)
    sib_near(3, gbuf)
    key_grads(LEFT)
    take_in(0)
    share_out(1, xc, sum_of(0))
    key_grads(RIGHT)
    sib_far(2, qbuf)
    sib_far(3, gbuf)
    for half in range(2):
        ys = (2 * half, 2 * half + 1)
        key_grads(DIAG, ys)
        for y in ys:
            out_v[y] = acc_v[y].astype(BF16)
            out_k[y] = (acc_k[y] * 0.5).astype(BF16)
        give_back(3, out_v, dv_ref, ys)
        give_back(2, out_k, dk_ref, ys)

    take_in(1)
    share_out(2, z, sum_of(1))

    for h in range(4):
        arrived(nrmbuf.at[h], ret_sems.at[0, h])
        cols = slice(h * 128, (h + 1) * 128)
        gated_vm[:, cols] = (nrmbuf[h].astype(F32) * gates_vm[:, cols].astype(F32)).astype(BF16)
    outproj_vm[...] = dot_nn(gated_vm[...], proj_vm[...]).astype(BF16)
    out_copy = pltpu.make_async_copy(outproj_vm, projected_ref.at[0], local_sems.at[3])
    out_copy.start()

    take_in(2)
    sums = sum_of(2)
    for h in range(4):
        bias_ref[h : h + 1, :] = sums[:, 16 * h : 16 * h + 16]

    for a, out_ref in ((1, dq_ref), (3, dv_ref), (2, dk_ref)):
        for h in range(4):
            arrived(out_ref.at[0, :, h * 128 : (h + 1) * 128], ret_sems.at[a, h])
    out_copy.wait()
    for copy in pending:
        copy.wait_send()


def hand_out(*refs):
    for i in range(5):
        refs[5 + i][...] = refs[i][...]


def shards(queries, keys, values, gates, out_proj, out_grad, lengths, rel_bias):
    anywhere = pl.BlockSpec(memory_space=pl.ANY)
    whole = pl.BlockSpec(memory_space=pltpu.VMEM)
    shape = jax.ShapeDtypeStruct
    head_rows = pltpu.VMEM((4, 8, 128, 128), BF16)
    own_rows = pltpu.VMEM((4, 128, 128), BF16)
    own_sums = pltpu.VMEM((4, 128, 128), F32)
    tables = pltpu.VMEM((4, 128, 256), F32)
    dma = pltpu.SemaphoreType.DMA
    made = (
            shape((1, 128, 1024), BF16),
            shape((1, 128, 512), BF16),
            shape((1, 128, 512), BF16),
            shape((1, 128, 512), BF16),
            shape((4, 16), F32),
        )
    results = pl.pallas_call(
        kernel,
        out_shape=made,
        in_specs=[anywhere] * 8,
        out_specs=(anywhere, anywhere, anywhere, anywhere, whole),
        scratch_shapes=[
            head_rows, head_rows, head_rows, head_rows,
            own_sums, own_sums, own_rows, own_rows,
            pltpu.VMEM((8, 128), F32), pltpu.VMEM((8, 128), F32),
            pltpu.VMEM((128, 1024), BF16),
            pltpu.VMEM((128, 512), BF16),
            pltpu.VMEM((512, 1024), BF16),
            pltpu.VMEM((128, 512), BF16),
            pltpu.VMEM((128, 1024), BF16),
            pltpu.VMEM((30, 128, 256), F32), pltpu.VMEM((4, 128, 256), F32),
            tables, tables, tables, tables,
            own_sums, own_sums, own_sums, own_sums,
            own_rows, own_rows, own_rows,
            tables, pltpu.VMEM((5, 8, 256), F32),
            pltpu.VMEM((3, 8, 1, 128), F32),
            pltpu.SMEM((1, 4), jnp.int32), pltpu.SMEM((4, 16), F32),
            dma((116,)), dma((4, 4)), dma((4, 14)), dma((4, 4)), dma((3, 8)), dma((1,)), dma((6,)),
        ],
        compiler_params=pltpu.CompilerParams(
            collective_id=0, has_side_effects=True, vmem_limit_bytes=60 * 2**20
        ),
    )(queries, keys, values, gates, out_proj, out_grad, lengths, rel_bias)
    return pl.pallas_call(
        hand_out,
        out_shape=made,
        in_specs=[whole] * 5,
        out_specs=(whole,) * 5,
    )(*results)


def solution(mesh):
    rows = P("dp", "seq", None)
    return jax.shard_map(
        shards,
        mesh=mesh,
        in_specs=(rows, rows, rows, rows, P(), rows, P("dp", None), P()),
        out_specs=(rows, rows, rows, rows, P()),
        check_vma=False,
    )
```
